32 devices in a mesh: rec: 2 (over y), leaf: 4 (over z), rhs: 2 (over x), pan: 2 (over core).
Axes of the slice: x: 2, y: 2, z: 4, core: 2. Of those that a mesh axis runs over, the one named last changes fastest.
Arguments:
- bottom_source: bfloat16 [32768, 256], P(('rec', 'leaf', 'rhs', 'pan')), parts along dimension 0, may hold values from -6 to 6
- bottom_inverse: bfloat16 [32768, 1024], P(('rec', 'leaf', 'rhs', 'pan')), parts along dimension 0, as said below
- bottom_update: bfloat16 [4096, 1024], P(('rec', 'leaf', 'rhs', 'pan')), parts along dimension 0, may hold values from -0.0625 to 0.0625
- bottom_sensitivity: bfloat16 [1024, 16384], P('rec', ('leaf', 'rhs', 'pan')), parts along dimension 0, may hold values from -0.03125 to 0.03125
- bottom_order: int32 [16, 1024], P(('leaf', 'rhs', 'pan')), may hold values from 0 to 1023, each once within a row
- bottom_extent: int32 [16], P(('leaf', 'rhs', 'pan')), may hold values from 384 to 1024, as said below
- bottom_targets: int32 [16, 128], P(('leaf', 'rhs', 'pan')), may hold values from 0 to 255, as said below
- upper_source: bfloat16 [3584, 256], P(('rec', 'leaf'), ('rhs', 'pan')), parts along dimension 0, may hold values from -6 to 6
- upper_inverse: bfloat16 [3584, 256], P(('rec', 'leaf')), parts along dimension 0, as said below
- upper_update: bfloat16 [256, 1536], P('rec', 'leaf'), parts along dimension 0, may hold values from -0.25 to 0.25
- upper_targets: int32 [6, 128], replicated, may hold values from 0 to 255, as said below
Outputs:
- adjoint: bfloat16 [32768, 256], P(('rec', 'leaf', 'rhs', 'pan')), parts along dimension 0
- gradient: float32 [1024, 256], P(('rec', 'leaf', 'rhs', 'pan')), parts along dimension 0
The draws below stay inside these ranges and needn't reach their ends.
There are 2 independent parts, one for each index of `rec`. The reference program is written for one: setup_inputs(seed, part) draws one part's arguments, and reference() takes and returns one part's arrays. A program takes and returns all parts, laid end to end along the dimension named above; an argument that names none is the same for every part. Nothing has to cross between parts.
Inputs may be any that keep to these rules, and one draw needn't show every extreme that they name: `bottom_inverse`: lower triangular, with its diagonal between 0.6 and 1.4. `upper_inverse`: lower triangular in each front's row order, with its diagonal between 0.6 and 1.4. `bottom_extent`: a multiple of 128; some front uses all 1024 rows. `bottom_targets`: the rows of one front go to distinct rows. `upper_targets`: the rows of one front go to distinct rows.
All inputs are finite; a program needn't handle non-finite values.
Results may differ from the reference program's by a relative error of at most 0.0058.
Values may be sent and summed in bfloat16 or wider, within the bound.
A program may use at most 64 MiB of HBM per device.

```python
import math
import jax
import jax.numpy as jnp
from jax import lax

NRHS = 256
BLK = 128
FB = 8
PU = 256
CR = 128
CRU = 128
NP = 512
PB = 1024
LEAVES = 4
MEMBERS = 4
NBF = 16
DEPTH = 2
UROWS = 448
UCROWS = 384
UPFRONTS = 6
MINB = 3


def triangle(key, row_index, order_size):
    columns = jnp.arange(order_size, dtype=jnp.int32)[None, :]
    row_grid = row_index[:, None]
    first_key, second_key = jax.random.split(key)
    shape_full = (row_index.shape[0], order_size)
    diagonal = jax.random.uniform(first_key, shape_full, jnp.float32, 0.8, 1.2)
    spread_part = jax.random.normal(second_key, shape_full, jnp.float32)
    lower_part = jnp.where(columns < row_grid, spread_part * (0.6 / math.sqrt(order_size)), 0.0)
    return jnp.where(columns == row_grid, diagonal, lower_part).astype(jnp.bfloat16)


def draw_bottom_inverse(key, part):
    row_index = jnp.arange(NBF * PB, dtype=jnp.int32) % PB
    return triangle(key, row_index, PB)


def draw_upper_inverse(key, part):
    position = jnp.arange(LEAVES * UROWS, dtype=jnp.int32)
    holder = position // UROWS
    inner_row = position % UROWS
    front_row = jnp.zeros((LEAVES * UROWS,), jnp.int32)
    for height in range(DEPTH + 1):
        row_count = PU >> height
        offset = 2 * PU - (2 * PU >> height)
        inside = (inner_row >= offset) & (inner_row < offset + row_count)
        front_row = jnp.where(inside, holder % (1 << height) * row_count + inner_row - offset, front_row)
    return triangle(jax.random.fold_in(key, 3), front_row, PU)


def draw_bottom_extent(key, part):
    first_key, second_key = jax.random.split(key)
    blocks_drawn = jax.random.randint(first_key, (NBF,), MINB, FB + 1)
    fullest = jax.random.randint(second_key, (), 0, NBF)
    blocks_drawn = jnp.where(jnp.arange(NBF, dtype=jnp.int32) == fullest, FB, blocks_drawn)
    return (blocks_drawn * BLK).astype(jnp.int32)


def distinct_rows(key, front_count, row_count):
    key_list = jax.random.split(key, front_count)
    chosen = jax.vmap(lambda single: jax.random.permutation(single, PU)[:row_count])(key_list)
    return chosen.astype(jnp.int32)


def draw_bottom_targets(key, part):
    return distinct_rows(jax.random.fold_in(key, 11), NBF, CR)


def draw_upper_targets(key, part):
    return distinct_rows(jax.random.fold_in(key, 17), UPFRONTS, CRU)


def strengthened(result, rng, source, target, shards_of, factor):
    owner, partner = [(jnp.arange(result.shape[axis_at]) // (result.shape[axis_at] // shards_of)).reshape([-1 if axis == axis_at else 1 for axis in range(result.ndim)]) for axis_at in (source, target)]
    chosen = jax.random.permutation(rng, shards_of)[partner]
    strong = (owner == chosen) | (owner == (partner + shards_of // 2) % shards_of)
    return jnp.where(strong, factor * result, result)


def steps_of(rng, extent, cuts, low, largest):
    loudness, own = 1.0, jax.random.fold_in(rng, 6)
    for dim, blocks in cuts:
        draws = jnp.exp(jax.random.uniform(jax.random.fold_in(own, dim), (blocks,), jnp.float32, low / len(cuts), largest / len(cuts)))
        loudness = loudness * jnp.repeat(draws, extent[dim] // blocks).reshape([-1 if axis == dim else 1 for axis in range(len(extent))])
    return loudness


def normal_values(rng, dims, width, most, cuts=(), kind=jnp.bfloat16):
    level = steps_of(rng, dims, cuts, -0.22, 0.18) if cuts else 1.0
    drawn = jax.random.normal(rng, dims, jnp.float32) * width * level
    return jnp.minimum(jnp.maximum(drawn, -most), most).astype(kind)


def noise_with(stream_key, extent, scale, most, shards, heavy, held_as=jnp.bfloat16):
    result = scale * jax.random.normal(stream_key, extent, jnp.float32)
    if shards:
        result = result * steps_of(stream_key, extent, shards, -0.22, 0.18)
    return jnp.clip(strengthened(result, jax.random.fold_in(stream_key, 3), *heavy), -most, most).astype(held_as)


def setup_inputs(seed: int = 0, part: int = 0) -> dict:
    streams_of = jax.random.split(jax.random.key(seed), 12)
    own_keys = jax.random.split(jax.random.fold_in(streams_of[11], part), 12)
    bottom_source = normal_values(own_keys[0], (NBF * PB, NRHS), 1.0, 6.0, ((0, 16),))
    bottom_inverse = draw_bottom_inverse(jax.random.fold_in(jax.random.fold_in(streams_of[11], part), 71), part)
    bottom_update = normal_values(own_keys[2], (NBF * CR, PB), (8 * PB) ** -0.5, 0.0625, ((0, 16),))
    bottom_sensitivity = noise_with(own_keys[3], (NP, NBF * PB), (64 * PB) ** -0.5, 0.03125, ((1, 16),), (1, 0, 16, 2.0))
    bottom_order = jax.vmap(lambda own: jax.random.permutation(own, PB))(jax.random.split(streams_of[4], NBF)).reshape((NBF, PB)).astype(jnp.int32)
    bottom_extent = draw_bottom_extent(jax.random.fold_in(streams_of[11], 71), part)
    bottom_targets = draw_bottom_targets(jax.random.fold_in(streams_of[11], 71), part)
    upper_source = normal_values(own_keys[7], (LEAVES * UROWS, NRHS), 1.0, 6.0, ((0, 4), (1, 4)))
    upper_inverse = draw_upper_inverse(jax.random.fold_in(jax.random.fold_in(streams_of[11], part), 71), part)
    upper_update = normal_values(own_keys[9], (CRU, LEAVES * UCROWS), (2 * PU) ** -0.5, 0.25, ((1, 4),))
    upper_targets = draw_upper_targets(jax.random.fold_in(streams_of[11], 71), part)
    return {"bottom_source": bottom_source, "bottom_inverse": bottom_inverse, "bottom_update": bottom_update, "bottom_sensitivity": bottom_sensitivity, "bottom_order": bottom_order, "bottom_extent": bottom_extent, "bottom_targets": bottom_targets, "upper_source": upper_source, "upper_inverse": upper_inverse, "upper_update": upper_update, "upper_targets": upper_targets}


def rounded(values):
    return lax.optimization_barrier(values.astype(jnp.bfloat16))


def widen(values):
    return values.astype(jnp.float32)


def level_rows(packed, height):
    column_count = packed.shape[1]
    grouped = packed.reshape(LEAVES, UROWS, column_count)
    offset = 2 * PU - (2 * PU >> height)
    row_count = PU >> height
    return grouped[:, offset:offset + row_count, :].reshape(LEAVES >> height, PU, column_count)


def level_columns(packed, height):
    grouped = packed.reshape(CRU, LEAVES, UCROWS)
    offset = 2 * PU - (2 * PU >> height)
    row_count = PU >> height
    chosen = grouped[:, :, offset:offset + row_count].reshape(CRU, LEAVES >> height, PU)
    return jnp.transpose(chosen, (1, 0, 2))


def level_targets(upper_targets, height):
    first_row = 2 * LEAVES - (2 * LEAVES >> height)
    return upper_targets[first_row:first_row + (LEAVES >> height)]


def spread_rows(contrib, targets):
    return jnp.zeros((PU, contrib.shape[1]), jnp.float32).at[targets].set(contrib)


def pick_rows(values, targets):
    return values[targets]


def unpermute_rows(values, order_rows):
    return jnp.zeros_like(values).at[order_rows].set(values)


def reference(bottom_source, bottom_inverse, bottom_update, bottom_sensitivity, bottom_order, bottom_extent, bottom_targets, upper_source, upper_inverse, upper_update, upper_targets):
    row_index = jnp.arange(PB, dtype=jnp.int32)
    masks = (row_index[None, :] < bottom_extent[:, None]).astype(jnp.float32).reshape(LEAVES, MEMBERS, PB, 1)
    source_all = bottom_source.reshape(LEAVES, MEMBERS, PB, NRHS)
    inverse_all = bottom_inverse.reshape(LEAVES, MEMBERS, PB, PB)
    update_all = bottom_update.reshape(LEAVES, MEMBERS, CR, PB)
    order_all = bottom_order.reshape(LEAVES, MEMBERS, PB)
    target_all = bottom_targets.reshape(LEAVES, MEMBERS, CR)
    sense_all = jnp.transpose(bottom_sensitivity.reshape(NP, LEAVES, MEMBERS, PB), (1, 0, 2, 3))

    def climb_leaf(leaf_items):
        source_leaf, inverse_leaf, update_leaf, order_leaf, mask_leaf, target_leaf = leaf_items
        ordered = rounded(widen(jax.vmap(pick_rows)(source_leaf, order_leaf)) * mask_leaf)
        solved = rounded(jnp.einsum("bij,bjc->bic", widen(inverse_leaf), widen(ordered)) * mask_leaf)
        contrib = jnp.einsum("brj,bjc->brc", widen(update_leaf), widen(solved))
        summed = jnp.sum(jax.vmap(spread_rows)(contrib, target_leaf), axis=0)
        return solved, summed

    solved_all, totals = lax.map(climb_leaf, (source_all, inverse_all, update_all, order_all, masks, target_all))

    front_input = rounded(widen(level_rows(upper_source, 0)) - totals)
    solved_upper = []
    for height in range(DEPTH + 1):
        inverse_now = widen(level_rows(upper_inverse, height))
        solved_front = rounded(jnp.einsum("fij,fjc->fic", inverse_now, widen(front_input)))
        solved_upper.append(solved_front)
        if height < DEPTH:
            update_now = widen(level_columns(upper_update, height))
            lifted = jnp.einsum("frj,fjc->frc", update_now, widen(solved_front))
            spread = jax.vmap(spread_rows)(lifted, level_targets(upper_targets, height))
            sibling_sum = spread.reshape(LEAVES >> (height + 1), 2, PU, NRHS).sum(axis=1)
            front_input = rounded(widen(level_rows(upper_source, height + 1)) - sibling_sum)

    back_rows = None
    for height in range(DEPTH, -1, -1):
        inverse_now = widen(level_rows(upper_inverse, height))
        if height == DEPTH:
            residue = solved_upper[height]
        else:
            parents = jnp.repeat(back_rows, 2, axis=0)
            picked = jax.vmap(pick_rows)(parents, level_targets(upper_targets, height))
            update_now = widen(level_columns(upper_update, height))
            residue = rounded(widen(solved_upper[height]) - jnp.einsum("frj,frc->fjc", update_now, widen(picked)))
        back_rows = rounded(jnp.einsum("fij,fic->fjc", inverse_now, widen(residue)))

    def descend_leaf(leaf_items):
        back_leaf, solved_leaf, inverse_leaf, update_leaf, order_leaf, mask_leaf, target_leaf, sense_leaf = leaf_items
        picked = back_leaf[target_leaf]
        residue = rounded((widen(solved_leaf) - jnp.einsum("brj,brc->bjc", widen(update_leaf), widen(picked))) * mask_leaf)
        bottom_back = rounded(jnp.einsum("bij,bic->bjc", widen(inverse_leaf), widen(residue)) * mask_leaf)
        adjoint_leaf = jax.vmap(unpermute_rows)(bottom_back, order_leaf)
        gradient_leaf = jnp.einsum("kbj,bjc->kc", widen(sense_leaf), widen(adjoint_leaf))
        return adjoint_leaf, gradient_leaf

    adjoints, gradients = lax.map(descend_leaf, (back_rows, solved_all, inverse_all, update_all, order_all, masks, target_all, sense_all))
    return adjoints.reshape(NBF * PB, NRHS), -jnp.sum(gradients, axis=0)
```

```python
import functools

import jax
import jax.numpy as jnp
from jax import lax
from jax.experimental import pallas as pl
from jax.experimental.pallas import tpu as pltpu
from jax.sharding import PartitionSpec as P

MESH = pl.DeviceIdType.MESH
F32 = jnp.float32
BF16 = jnp.bfloat16
LANES = 128
PLAIN = ((1,), (0,))
RIGHT_T = ((1,), (1,))
LEFT_T = ((0,), (0,))


def mul(a, b, dims=PLAIN):
    return lax.dot_general(a, b, (dims, ((), ())), preferred_element_type=F32)


def one_hot(rows, keys):
    shape = (rows, keys.shape[1])
    hit = lax.broadcasted_iota(jnp.int32, shape, 0) == keys
    return jnp.where(hit, 1.0, 0.0).astype(BF16)


def kernel(
    sizes,
    src_h, inv_h, upd_h, sen_h, ord_h, ext_h, tgt_h, us_h, ui_h, uc_h, ut_h,
    adj_h, grad_ref,
    src, inv, upd, sen, order, extent, target, us0, ui, uc, ut,
    local_sem,
    nhot, spread_upd, solved, ordered, adj,
    hi, us, iv, cp, ld, zed,
    sp, pr, lf, ba, back_own, gs, gr, gh, gz,
    hi_s, hi_r, rel_s, rel_r, us_s, us_r, pr_s, pr_r, lf_s, lf_r, ba_s, ba_r, gr_s, gr_r, gz_s, gz_r,
):
    leaves, rhs, pan, front, rows_each = sizes
    members = rhs * pan
    depth = leaves.bit_length() - 1
    rows = inv.shape[0]
    width = us.shape[2]
    f = lax.axis_index("leaf")
    x = lax.axis_index("rhs")
    c = lax.axis_index("pan")
    j = x * pan + c
    half = front // 2
    inv_rows = ui.shape[0] - front
    cut = uc.shape[0] // 2
    strips = (hi.shape[1] - inv_rows) // cut
    upper_cols = uc.shape[1] - front

    def member(k):
        return lax.rem(j + k, members)

    def leaf(k):
        return lax.rem(f + k, leaves)

    def at_member(k):
        place = member(k)
        return {"rhs": place // pan, "pan": lax.rem(place, pan)}

    def at_leaf(k):
        return {"leaf": leaf(k)}

    def copy(a, b, s, r, to):
        return pltpu.make_async_remote_copy(
            src_ref=a, dst_ref=b, send_sem=s, recv_sem=r, device_id=to, device_id_type=MESH
        )

    fetch = {}
    for place, (name, a, b) in enumerate((
        ("ui", ui_h, ui), ("uc", uc_h, uc), ("order", ord_h, order), ("extent", ext_h, extent),
        ("target", tgt_h, target), ("ut", ut_h, ut), ("upd", upd_h, upd), ("src", src_h, src),
        ("inv", inv_h, inv), ("us0", us_h, us0), ("sen", sen_h, sen),
    )):
        fetch[name] = pltpu.make_async_copy(a, b, local_sem.at[place])
        fetch[name].start()

    barrier = pltpu.get_barrier_semaphore()
    for k in range(1, members):
        pl.semaphore_signal(barrier, inc=1, device_id=at_member(k), device_id_type=MESH)
    for k in range(1, leaves):
        pl.semaphore_signal(barrier, inc=1, device_id=at_leaf(k), device_id_type=MESH)
    pl.semaphore_wait(barrier, members + leaves - 2)

    fetch["ui"].wait()
    fetch["uc"].wait()
    for side in range(2):
        slot = side * leaves + f
        hi[slot, 0:inv_rows, :] = ui[front:, side * half : (side + 1) * half]
        for strip in range(strips):
            start = inv_rows + strip * cut
            have = min(LANES, upper_cols - strip * LANES)
            piece = uc[side * cut : (side + 1) * cut, front + strip * LANES : front + strip * LANES + have]
            if have < LANES:
                piece = jnp.concatenate([piece, jnp.zeros((cut, LANES - have), BF16)], axis=1)
            hi[slot, start : start + cut, :] = piece
    mine = c * leaves + f
    sends = []
    for k in range(1, leaves):
        out = copy(hi.at[mine], hi.at[mine], hi_s.at[k], hi_r.at[f], at_leaf(k))
        out.start()
        sends.append(out)
    fetch["us0"].wait()
    us[f] = us0[front:, :]
    for k in range(1, leaves):
        out = copy(us.at[f], us.at[f], us_s.at[k], us_r.at[f], at_leaf(k))
        out.start()
        sends.append(out)

    for name in ("order", "extent", "target", "ut"):
        fetch[name].wait()
    used = lax.broadcasted_iota(jnp.int32, (1, rows), 1) < extent[0]
    keys = jnp.where(used, order[...], -1)
    for start in range(0, rows, 256):
        hit = lax.broadcasted_iota(jnp.int32, (256, rows), 0) + start == keys
        nhot[start : start + 256, :] = jnp.where(hit, 1.0, 0.0).astype(BF16)
    fetch["src"].wait()
    ordered[...] = mul(src[...], nhot[...], LEFT_T).astype(BF16)
    fetch["upd"].wait()
    spread_upd[...] = mul(one_hot(front, target[...]), upd[...]).astype(BF16)
    fetch["inv"].wait()
    for start in range(0, rows, 256):
        end = start + 256
        block = mul(ordered[:, :end], inv[start:end, :end], RIGHT_T)
        solved[:, start:end] = jnp.where(used[:, start:end], block, 0.0).astype(BF16)
    sp[...] = mul(solved[...], spread_upd[...], RIGHT_T).astype(BF16)
    for k in range(1, members):
        to = pl.multiple_of(member(k) * width, width)
        out = copy(sp.at[pl.ds(to, width)], pr.at[j], pr_s.at[k], pr_r.at[j], at_member(k))
        out.start()
        sends.append(out)
    pr[j] = sp[pl.ds(pl.multiple_of(j * width, width), width), :]

    eye = one_hot(front, lax.broadcasted_iota(jnp.int32, (1, front), 1))
    load_own = mul(us0[:front, :], eye, LEFT_T)
    map_own = one_hot(front, ut[pl.ds(f, 1), :])
    cp_own = mul(map_own, uc[:, :front]).astype(BF16)
    inv_own = ui[:front, :]

    for k in range(1, members):
        place = member(k)
        copy(pr.at[place], pr.at[place], pr_s.at[k], pr_r.at[place], at_member(k)).wait_recv()
    total = pr[0].astype(F32)
    for place in range(1, members):
        total = total + pr[place].astype(F32)
    front_in = (load_own - total).astype(BF16)
    zed_own = mul(front_in, inv_own, RIGHT_T).astype(BF16)
    lf[f] = mul(zed_own, cp_own, RIGHT_T).astype(BF16)
    for k in range(1, leaves):
        out = copy(lf.at[f], lf.at[f], lf_s.at[k], lf_r.at[f], at_leaf(k))
        out.start()
        sends.append(out)

    for k in range(1, leaves):
        slot = c * leaves + leaf(k)
        copy(hi.at[slot], hi.at[slot], hi_s.at[k], hi_r.at[leaf(k)], at_leaf(k)).wait_recv()
        out = copy(hi.at[slot], hi.at[slot], rel_s.at[k], rel_r.at[leaf(k)], {"pan": 1 - c})
        out.start()
        sends.append(out)
    for k in range(1, leaves):
        slot = leaf(k)
        copy(us.at[slot], us.at[slot], us_s.at[k], us_r.at[slot], at_leaf(k)).wait_recv()
    for k in range(1, leaves):
        slot = (1 - c) * leaves + leaf(k)
        copy(hi.at[slot], hi.at[slot], rel_s.at[k], rel_r.at[leaf(k)], {"pan": 1 - c}).wait_recv()

    first = {}
    count = 0
    for height in range(1, depth + 1):
        first[height] = count
        count += leaves >> height
    for height in range(1, depth + 1):
        n = front >> height
        o = front - (2 * front >> height)
        for p in range(leaves >> height):
            at = first[height] + p
            group = [p * (1 << height) + s for s in range(1 << height)]
            for s, g in enumerate(group):
                for side in range(2):
                    iv[at, s * n : (s + 1) * n, side * half : (side + 1) * half] = hi[
                        side * leaves + g, o : o + n, :
                    ]
            stacked = jnp.concatenate([us[g, o : o + n, :] for g in group], axis=0)
            ld[at] = mul(stacked, eye, LEFT_T)
            if height < depth:
                pieces = []
                for s, g in enumerate(group):
                    strip_list = [
                        jnp.concatenate(
                            [
                                hi[side * leaves + g, inv_rows + strip * cut : inv_rows + (strip + 1) * cut, :]
                                for side in range(2)
                            ],
                            axis=0,
                        )
                        for strip in range(strips)
                    ]
                    if n % LANES == 0 and o % LANES == 0:
                        pieces.extend(strip_list[o // LANES : (o + n) // LANES])
                    else:
                        whole = jnp.concatenate(strip_list, axis=1)
                        line = lax.broadcasted_iota(jnp.int32, (1, front), 1) - s * n
                        line = jnp.where((line >= 0) & (line < n), line + o, -1)
                        part = mul(whole, one_hot(whole.shape[1], line))
                        pieces = [part + pieces[0]] if pieces else [part]
                coup = jnp.concatenate(pieces, axis=1) if len(pieces) > 1 else pieces[0]
                map_row = 2 * leaves - (2 * leaves >> height) + p
                cp[at] = mul(one_hot(front, ut[map_row : map_row + 1, :]), coup.astype(BF16)).astype(BF16)

    for k in range(1, leaves):
        slot = leaf(k)
        copy(lf.at[slot], lf.at[slot], lf_s.at[k], lf_r.at[slot], at_leaf(k)).wait_recv()
    lifts = [lf[g].astype(F32) for g in range(leaves)]
    for height in range(1, depth + 1):
        above = []
        for p in range(leaves >> height):
            at = first[height] + p
            now = (ld[at] - (lifts[2 * p] + lifts[2 * p + 1])).astype(BF16)
            value = mul(now, iv[at], RIGHT_T).astype(BF16)
            zed[at] = value
            if height < depth:
                above.append(mul(value, cp[at], RIGHT_T))
        lifts = above
    back = mul(zed[first[depth]], iv[first[depth]]).astype(BF16)
    for height in range(depth - 1, 0, -1):
        at = first[height] + f // (1 << height)
        residue = (zed[at].astype(F32) - mul(back, cp[at])).astype(BF16)
        back = mul(residue, iv[at]).astype(BF16)
    residue = (zed_own.astype(F32) - mul(back, cp_own)).astype(BF16)
    back_own[...] = mul(residue, inv_own).astype(BF16)
    own_rows = pl.ds(pl.multiple_of(j * width, width), width)
    for k in range(1, members):
        out = copy(back_own, ba.at[own_rows], ba_s.at[k], ba_r.at[j], at_member(k))
        out.start()
        sends.append(out)
    ba[own_rows, :] = back_own[...]
    for k in range(1, members):
        place = member(k)
        here = ba.at[pl.ds(pl.multiple_of(place * width, width), width)]
        copy(here, here, ba_s.at[k], ba_r.at[place], at_member(k)).wait_recv()

    for start in range(0, rows, 256):
        end = start + 256
        value = solved[:, start:end].astype(F32) - mul(ba[...], spread_upd[:, start:end])
        ordered[:, start:end] = jnp.where(used[:, start:end], value, 0.0).astype(BF16)
    for start in range(0, rows, 256):
        end = start + 256
        block = mul(ordered[:, start:], inv[start:, start:end])
        solved[:, start:end] = jnp.where(used[:, start:end], block, 0.0).astype(BF16)
    adj[...] = mul(nhot[...], solved[...], RIGHT_T).astype(BF16)
    store = pltpu.make_async_copy(adj, adj_h, local_sem.at[11])
    store.start()
    fetch["sen"].wait()
    grad = -mul(sen[...], adj[...])
    tail = gs.shape[2] - rows_each
    for place in range(members):
        for g in range(leaves):
            start = (g * members + place) * rows_each
            piece = grad[start : start + rows_each]
            if tail:
                piece = jnp.concatenate([piece, jnp.zeros((tail, piece.shape[1]), F32)], axis=0)
            gs[place, g] = piece.astype(BF16)
    for k in range(1, members):
        out = copy(gs.at[member(k)], gr.at[j], gr_s.at[k], gr_r.at[j], at_member(k))
        out.start()
        sends.append(out)
    gr[j] = gs[j]
    for k in range(1, members):
        place = member(k)
        copy(gr.at[place], gr.at[place], gr_s.at[k], gr_r.at[place], at_member(k)).wait_recv()
    summed = gr[0].astype(F32)
    for place in range(1, members):
        summed = summed + gr[place].astype(F32)
    gh[...] = summed
    for k in range(1, leaves):
        out = copy(gh.at[leaf(k)], gz.at[f], gz_s.at[k], gz_r.at[f], at_leaf(k))
        out.start()
        sends.append(out)
    gz[f] = gh[f]
    for k in range(1, leaves):
        slot = leaf(k)
        copy(gz.at[slot], gz.at[slot], gz_s.at[k], gz_r.at[slot], at_leaf(k)).wait_recv()
    summed = gz[0]
    for g in range(1, leaves):
        summed = summed + gz[g]
    grad_ref[...] = summed[:rows_each]
    for out in sends:
        out.wait_send()
    store.wait()


def shards(*arrays):
    (src, inv, upd, sen, order, extent, target, us, ui, uc, ut) = arrays
    leaves, rhs, pan = (lax.axis_size(name) for name in ("leaf", "rhs", "pan"))
    members = rhs * pan
    front = ui.shape[1]
    rows, cols = src.shape
    width = cols // members
    rows_each = sen.shape[0] // (leaves * members)
    rows_kept = -(-rows_each // 16) * 16
    upper_rows = ui.shape[0] - front
    strips = -(-(uc.shape[1] - front) // LANES)
    hi_rows = upper_rows + strips * (uc.shape[0] // 2)
    above = leaves - 1

    def room(shape, kind=BF16):
        return pltpu.VMEM(shape, kind)

    scratch = [
        room(src.shape), room(inv.shape), room(upd.shape), room(sen.shape),
        room(order.shape, jnp.int32), pltpu.SMEM(extent.shape, jnp.int32), room(target.shape, jnp.int32),
        room(us.shape), room(ui.shape), room(uc.shape), room(ut.shape, jnp.int32),
        pltpu.SemaphoreType.DMA((12,)),
        room((rows, rows)), room((front, rows)), room((cols, rows)), room((cols, rows)), room((rows, cols)),
        room((2 * leaves, hi_rows, LANES)), room((leaves, upper_rows, width)),
        room((above, front, front)), room((above, front, front)),
        room((above, width, front), F32), room((above, width, front)),
        room((cols, front)), room((members, width, front)), room((leaves, width, front)),
        room((cols, front)), room((width, front)),
        room((members, leaves, rows_kept, cols)), room((members, leaves, rows_kept, cols)),
        room((leaves, rows_kept, cols), F32), room((leaves, rows_kept, cols), F32),
    ]
    for count in (leaves, leaves, leaves, members, leaves, members, members, leaves):
        scratch += [pltpu.SemaphoreType.DMA((count,))] * 2
    any_spec = pl.BlockSpec(memory_space=pl.ANY)
    flops = 2 * rows * rows * cols * 4
    return pl.pallas_call(
        functools.partial(kernel, (leaves, rhs, pan, front, rows_each)),
        out_shape=(
            jax.ShapeDtypeStruct(src.shape, BF16),
            jax.ShapeDtypeStruct((rows_each, cols), F32),
        ),
        in_specs=[any_spec] * 11,
        out_specs=(any_spec, pl.BlockSpec(memory_space=pltpu.VMEM)),
        scratch_shapes=scratch,
        compiler_params=pltpu.CompilerParams(
            collective_id=0, has_side_effects=True, vmem_limit_bytes=56 * 2**20
        ),
        cost_estimate=pl.CostEstimate(flops=flops, bytes_accessed=5 * 2**20, transcendentals=0),
    )(*arrays)


def solution(mesh):
    placed = (
        P(("rec", "leaf", "rhs", "pan"), None),
        P(("rec", "leaf", "rhs", "pan"), None),
        P(("rec", "leaf", "rhs", "pan"), None),
        P("rec", ("leaf", "rhs", "pan")),
        P(("leaf", "rhs", "pan"), None),
        P(("leaf", "rhs", "pan")),
        P(("leaf", "rhs", "pan"), None),
        P(("rec", "leaf"), ("rhs", "pan")),
        P(("rec", "leaf"), None),
        P("rec", "leaf"),
        P(),
    )
    return jax.shard_map(
        shards,
        mesh=mesh,
        in_specs=placed,
        out_specs=(P(("rec", "leaf", "rhs", "pan"), None), P(("rec", "leaf", "rhs", "pan"), None)),
        check_vma=False,
    )
```

```python
import functools

import jax
import jax.numpy as jnp
from jax import lax
from jax.experimental import pallas as pl
from jax.experimental.pallas import tpu as pltpu
from jax.sharding import PartitionSpec as P

MESH = pl.DeviceIdType.MESH
F32 = jnp.float32
BF16 = jnp.bfloat16
LANES = 128
PLAIN = ((1,), (0,))
RIGHT_T = ((1,), (1,))
LEFT_T = ((0,), (0,))


def mul(a, b, dims=PLAIN):
    return lax.dot_general(a, b, (dims, ((), ())), preferred_element_type=F32)


def one_hot(rows, keys):
    shape = (rows, keys.shape[1])
    hit = lax.broadcasted_iota(jnp.int32, shape, 0) == keys
    return jnp.where(hit, 1.0, 0.0).astype(BF16)


def kernel(
    sizes,
    src_h, inv_h, upd_h, sen_h, ord_h, ext_h, tgt_h, us_h, ui_h, uc_h, ut_h,
    adj_h, grad_ref,
    src, inv, upd, sen, order, extent, target, us0, ui, uc, ut,
    local_sem,
    nhot, spread_upd, solved, ordered, adj,
    hi, us, iv, cp, ld, zed,
    sp, pr, lf, ba, back_own, gs, gr, gh, gz,
    hi_s, hi_r, row_s, row_r, rel_s, rel_r, us_s, us_r, pr_s, pr_r, lf_s, lf_r, ba_s, ba_r, gr_s, gr_r, gz_s, gz_r,
):
    leaves, rhs, pan, front, rows_each = sizes
    members = rhs * pan
    depth = leaves.bit_length() - 1
    rows = inv.shape[0]
    width = us.shape[1]
    f = lax.axis_index("leaf")
    x = lax.axis_index("rhs")
    c = lax.axis_index("pan")
    j = x * pan + c
    half = front // 2
    inv_rows = ui.shape[0] - front
    cut = uc.shape[0] // 2
    upper_cols = uc.shape[1] - front
    strips = -(-upper_cols // LANES)
    part = hi.shape[1] // rhs

    def member(k):
        return lax.rem(j + k, members)

    def leaf(k):
        return lax.rem(f + k, leaves)

    def at_member(k):
        place = member(k)
        return {"rhs": place // pan, "pan": lax.rem(place, pan)}

    def at_leaf(k):
        return {"leaf": leaf(k)}

    def copy(a, b, s, r, to):
        return pltpu.make_async_remote_copy(
            src_ref=a, dst_ref=b, send_sem=s, recv_sem=r, device_id=to, device_id_type=MESH
        )

    fetch = {}
    for place, (name, a, b) in enumerate((
        ("ui", ui_h, ui), ("uc", uc_h, uc), ("order", ord_h, order), ("extent", ext_h, extent),
        ("target", tgt_h, target), ("ut", ut_h, ut), ("upd", upd_h, upd), ("src", src_h, src),
        ("inv", inv_h, inv), ("us0", us_h, us0), ("sen", sen_h, sen),
    )):
        fetch[name] = pltpu.make_async_copy(a, b, local_sem.at[place])
        fetch[name].start()

    barrier = pltpu.get_barrier_semaphore()
    for k in range(1, members):
        pl.semaphore_signal(barrier, inc=1, device_id=at_member(k), device_id_type=MESH)
    for k in range(1, leaves):
        pl.semaphore_signal(barrier, inc=1, device_id=at_leaf(k), device_id_type=MESH)
    pl.semaphore_wait(barrier, members + leaves - 2)

    fetch["ui"].wait()
    fetch["uc"].wait()
    for side in range(2):
        slot = side * leaves + f
        hi[slot, 0:inv_rows, :] = ui[front:, side * half : (side + 1) * half]
        for strip in range(strips):
            start = inv_rows + strip * cut
            have = min(LANES, upper_cols - strip * LANES)
            piece = uc[side * cut : (side + 1) * cut, front + strip * LANES : front + strip * LANES + have]
            if have < LANES:
                piece = jnp.concatenate([piece, jnp.zeros((cut, LANES - have), BF16)], axis=1)
            hi[slot, start : start + cut, :] = piece
        start = inv_rows + strips * cut
        if start < hi.shape[1]:
            hi[slot, start:, :] = jnp.zeros((hi.shape[1] - start, LANES), BF16)
    sends = []

    def share(place):
        return hi.at[c * leaves + place, pl.ds(pl.multiple_of(x * part, part), part)]

    for k in range(1, leaves):
        out = copy(share(f), share(f), hi_s.at[k], hi_r.at[f], at_leaf(k))
        out.start()
        sends.append(out)
    fetch["us0"].wait()
    us[f] = us0[:, front:]
    for k in range(1, leaves):
        out = copy(us.at[f], us.at[f], us_s.at[k], us_r.at[f], at_leaf(k))
        out.start()
        sends.append(out)

    for name in ("order", "extent", "target", "ut"):
        fetch[name].wait()
    used = lax.broadcasted_iota(jnp.int32, (1, rows), 1) < extent[0]
    keys = jnp.where(used, order[...], -1)
    for start in range(0, rows, 256):
        hit = lax.broadcasted_iota(jnp.int32, (256, rows), 0) + start == keys
        nhot[start : start + 256, :] = jnp.where(hit, 1.0, 0.0).astype(BF16)
    fetch["src"].wait()
    ordered[...] = mul(src[...], nhot[...], LEFT_T).astype(BF16)
    fetch["upd"].wait()
    spread_upd[...] = mul(one_hot(front, target[...]), upd[...]).astype(BF16)
    fetch["inv"].wait()
    for start in range(0, rows, 256):
        end = start + 256
        block = mul(ordered[:, :end], inv[start:end, :end], RIGHT_T)
        solved[:, start:end] = jnp.where(used[:, start:end], block, 0.0).astype(BF16)
    sp[...] = mul(solved[...], spread_upd[...], RIGHT_T).astype(BF16)
    for k in range(1, members):
        to = pl.multiple_of(member(k) * width, width)
        out = copy(sp.at[pl.ds(to, width)], pr.at[j], pr_s.at[k], pr_r.at[j], at_member(k))
        out.start()
        sends.append(out)
    pr[j] = sp[pl.ds(pl.multiple_of(j * width, width), width), :]

    load_own = us0[:, :front].astype(F32)
    map_own = one_hot(front, ut[pl.ds(f, 1), :])
    cp_own = mul(map_own, uc[:, :front]).astype(BF16)
    inv_own = ui[:front, :]

    for k in range(1, leaves):
        g = leaf(k)
        copy(share(g), share(g), hi_s.at[k], hi_r.at[g], at_leaf(k)).wait_recv()
        for t in range(1, rhs):
            out = copy(share(g), share(g), row_s.at[t, k], row_r.at[x, g], {"rhs": lax.rem(x + t, rhs)})
            out.start()
            sends.append(out)

    for k in range(1, members):
        place = member(k)
        copy(pr.at[place], pr.at[place], pr_s.at[k], pr_r.at[place], at_member(k)).wait_recv()
    total = pr[0].astype(F32)
    for place in range(1, members):
        total = total + pr[place].astype(F32)
    front_in = (load_own - total).astype(BF16)
    zed_own = mul(front_in, inv_own, RIGHT_T).astype(BF16)
    lf[f] = mul(zed_own, cp_own, RIGHT_T).astype(BF16)
    for k in range(1, leaves):
        out = copy(lf.at[f], lf.at[f], lf_s.at[k], lf_r.at[f], at_leaf(k))
        out.start()
        sends.append(out)

    for k in range(1, leaves):
        slot = c * leaves + leaf(k)
        for t in range(1, rhs):
            other = lax.rem(x + t, rhs)
            here = hi.at[slot, pl.ds(pl.multiple_of(other * part, part), part)]
            copy(here, here, row_s.at[t, k], row_r.at[other, leaf(k)], {"rhs": other}).wait_recv()
        out = copy(hi.at[slot], hi.at[slot], rel_s.at[k], rel_r.at[leaf(k)], {"pan": 1 - c})
        out.start()
        sends.append(out)
    for k in range(1, leaves):
        slot = leaf(k)
        copy(us.at[slot], us.at[slot], us_s.at[k], us_r.at[slot], at_leaf(k)).wait_recv()
    for k in range(1, leaves):
        slot = (1 - c) * leaves + leaf(k)
        copy(hi.at[slot], hi.at[slot], rel_s.at[k], rel_r.at[leaf(k)], {"pan": 1 - c}).wait_recv()

    first = {}
    count = 0
    for height in range(1, depth + 1):
        first[height] = count
        count += leaves >> height
    for height in range(1, depth + 1):
        n = front >> height
        o = front - (2 * front >> height)
        for p in range(leaves >> height):
            at = first[height] + p
            group = [p * (1 << height) + s for s in range(1 << height)]
            for s, g in enumerate(group):
                for side in range(2):
                    iv[at, s * n : (s + 1) * n, side * half : (side + 1) * half] = hi[
                        side * leaves + g, o : o + n, :
                    ]
            if n % LANES == 0 and o % LANES == 0:
                ld[at] = jnp.concatenate([us[g, :, o : o + n] for g in group], axis=1).astype(F32)
            else:
                load = jnp.zeros(ld.shape[1:], F32)
                for s, g in enumerate(group):
                    line = lax.broadcasted_iota(jnp.int32, (1, front), 1) - s * n
                    line = jnp.where((line >= 0) & (line < n), line + o, -1)
                    load = load + mul(us[g], one_hot(us.shape[2], line))
                ld[at] = load
            if height < depth:
                pieces = []
                for s, g in enumerate(group):
                    strip_list = [
                        jnp.concatenate(
                            [
                                hi[side * leaves + g, inv_rows + strip * cut : inv_rows + (strip + 1) * cut, :]
                                for side in range(2)
                            ],
                            axis=0,
                        )
                        for strip in range(strips)
                    ]
                    if n % LANES == 0 and o % LANES == 0:
                        pieces.extend(strip_list[o // LANES : (o + n) // LANES])
                    else:
                        whole = jnp.concatenate(strip_list, axis=1)
                        line = lax.broadcasted_iota(jnp.int32, (1, front), 1) - s * n
                        line = jnp.where((line >= 0) & (line < n), line + o, -1)
                        gain = mul(whole, one_hot(whole.shape[1], line))
                        pieces = [gain + pieces[0]] if pieces else [gain]
                coup = jnp.concatenate(pieces, axis=1) if len(pieces) > 1 else pieces[0]
                map_row = 2 * leaves - (2 * leaves >> height) + p
                cp[at] = mul(one_hot(front, ut[map_row : map_row + 1, :]), coup.astype(BF16)).astype(BF16)

    for k in range(1, leaves):
        slot = leaf(k)
        copy(lf.at[slot], lf.at[slot], lf_s.at[k], lf_r.at[slot], at_leaf(k)).wait_recv()
    lifts = [lf[g].astype(F32) for g in range(leaves)]
    for height in range(1, depth + 1):
        above = []
        for p in range(leaves >> height):
            at = first[height] + p
            now = (ld[at] - (lifts[2 * p] + lifts[2 * p + 1])).astype(BF16)
            value = mul(now, iv[at], RIGHT_T).astype(BF16)
            zed[at] = value
            if height < depth:
                above.append(mul(value, cp[at], RIGHT_T))
        lifts = above
    back = mul(zed[first[depth]], iv[first[depth]]).astype(BF16)
    for height in range(depth - 1, 0, -1):
        at = first[height] + f // (1 << height)
        residue = (zed[at].astype(F32) - mul(back, cp[at])).astype(BF16)
        back = mul(residue, iv[at]).astype(BF16)
    residue = (zed_own.astype(F32) - mul(back, cp_own)).astype(BF16)
    back_own[...] = mul(residue, inv_own).astype(BF16)
    own_rows = pl.ds(pl.multiple_of(j * width, width), width)
    for k in range(1, members):
        out = copy(back_own, ba.at[own_rows], ba_s.at[k], ba_r.at[j], at_member(k))
        out.start()
        sends.append(out)
    ba[own_rows, :] = back_own[...]
    for k in range(1, members):
        place = member(k)
        here = ba.at[pl.ds(pl.multiple_of(place * width, width), width)]
        copy(here, here, ba_s.at[k], ba_r.at[place], at_member(k)).wait_recv()

    for start in range(0, rows, 256):
        end = start + 256
        value = solved[:, start:end].astype(F32) - mul(ba[...], spread_upd[:, start:end])
        ordered[:, start:end] = jnp.where(used[:, start:end], value, 0.0).astype(BF16)
    for start in range(0, rows, 256):
        end = start + 256
        block = mul(ordered[:, start:], inv[start:, start:end])
        solved[:, start:end] = jnp.where(used[:, start:end], block, 0.0).astype(BF16)
    adj[...] = mul(nhot[...], solved[...], RIGHT_T).astype(BF16)
    store = pltpu.make_async_copy(adj, adj_h, local_sem.at[11])
    store.start()
    fetch["sen"].wait()
    grad = -mul(sen[...], adj[...])
    tail = gs.shape[2] - rows_each
    for place in range(members):
        for g in range(leaves):
            start = (g * members + place) * rows_each
            piece = grad[start : start + rows_each]
            if tail:
                piece = jnp.concatenate([piece, jnp.zeros((tail, piece.shape[1]), F32)], axis=0)
            gs[place, g] = piece.astype(BF16)
    for k in range(1, members):
        out = copy(gs.at[member(k)], gr.at[j], gr_s.at[k], gr_r.at[j], at_member(k))
        out.start()
        sends.append(out)
    gr[j] = gs[j]
    for k in range(1, members):
        place = member(k)
        copy(gr.at[place], gr.at[place], gr_s.at[k], gr_r.at[place], at_member(k)).wait_recv()
    summed = gr[0].astype(F32)
    for place in range(1, members):
        summed = summed + gr[place].astype(F32)
    gh[...] = summed.astype(BF16)
    for k in range(1, leaves):
        out = copy(gh.at[leaf(k)], gz.at[f], gz_s.at[k], gz_r.at[f], at_leaf(k))
        out.start()
        sends.append(out)
    gz[f] = gh[f]
    for k in range(1, leaves):
        slot = leaf(k)
        copy(gz.at[slot], gz.at[slot], gz_s.at[k], gz_r.at[slot], at_leaf(k)).wait_recv()
    summed = gz[0].astype(F32)
    for g in range(1, leaves):
        summed = summed + gz[g].astype(F32)
    grad_ref[...] = summed[:rows_each]
    for out in sends:
        out.wait_send()
    store.wait()


def hand_on(adj, grad, adj_out, grad_out, adj_held, grad_held, sem):
    step = adj.shape[0] // 4
    parts = [(grad, grad_held, grad_out)]
    for start in range(0, adj.shape[0], step):
        rows = pl.ds(start, step)
        parts.append((adj.at[rows], adj_held.at[rows], adj_out.at[rows]))
    moves = []
    for place, (a, b, to) in enumerate(parts):
        come = pltpu.make_async_copy(a, b, sem.at[0, place])
        come.start()
        moves.append((come, pltpu.make_async_copy(b, to, sem.at[1, place])))
    for come, go in moves:
        come.wait()
        go.start()
    for come, go in moves:
        go.wait()


def shards(*arrays):
    (src, inv, upd, sen, order, extent, target, us, ui, uc, ut) = arrays
    us = us.T
    leaves, rhs, pan = (lax.axis_size(name) for name in ("leaf", "rhs", "pan"))
    members = rhs * pan
    front = ui.shape[1]
    rows, cols = src.shape
    width = cols // members
    rows_each = sen.shape[0] // (leaves * members)
    rows_kept = -(-rows_each // 16) * 16
    upper_rows = ui.shape[0] - front
    strips = -(-(uc.shape[1] - front) // LANES)
    hi_rows = -(-(upper_rows + strips * (uc.shape[0] // 2)) // (16 * rhs)) * 16 * rhs
    above = leaves - 1

    def room(shape, kind=BF16):
        return pltpu.VMEM(shape, kind)

    scratch = [
        room(src.shape), room(inv.shape), room(upd.shape), room(sen.shape),
        room(order.shape, jnp.int32), pltpu.SMEM(extent.shape, jnp.int32), room(target.shape, jnp.int32),
        room(us.shape), room(ui.shape), room(uc.shape), room(ut.shape, jnp.int32),
        pltpu.SemaphoreType.DMA((12,)),
        room((rows, rows)), room((front, rows)), room((cols, rows)), room((cols, rows)), room((rows, cols)),
        room((2 * leaves, hi_rows, LANES)), room((leaves, width, upper_rows)),
        room((above, front, front)), room((above, front, front)),
        room((above, width, front), F32), room((above, width, front)),
        room((cols, front)), room((members, width, front)), room((leaves, width, front)),
        room((cols, front)), room((width, front)),
        room((members, leaves, rows_kept, cols)), room((members, leaves, rows_kept, cols)),
        room((leaves, rows_kept, cols)), room((leaves, rows_kept, cols)),
    ]
    for count in (leaves, (rhs, leaves), leaves, leaves, members, leaves, members, members, leaves):
        count = count if isinstance(count, tuple) else (count,)
        scratch += [pltpu.SemaphoreType.DMA(count)] * 2
    any_spec = pl.BlockSpec(memory_space=pl.ANY)
    flops = 2 * rows * rows * cols * 4
    held = pl.pallas_call(
        functools.partial(kernel, (leaves, rhs, pan, front, rows_each)),
        out_shape=(
            jax.ShapeDtypeStruct(src.shape, BF16),
            jax.ShapeDtypeStruct((rows_each, cols), F32),
        ),
        in_specs=[any_spec] * 11,
        out_specs=(any_spec, pl.BlockSpec(memory_space=pltpu.VMEM)),
        scratch_shapes=scratch,
        compiler_params=pltpu.CompilerParams(
            collective_id=0, has_side_effects=True, vmem_limit_bytes=56 * 2**20
        ),
        cost_estimate=pl.CostEstimate(flops=flops, bytes_accessed=5 * 2**20, transcendentals=0),
    )(src, inv, upd, sen, order, extent, target, us, ui, uc, ut)
    hbm = pl.BlockSpec(memory_space=pltpu.HBM)
    return pl.pallas_call(
        hand_on,
        out_shape=tuple(jax.ShapeDtypeStruct(part.shape, part.dtype) for part in held),
        in_specs=[hbm] * 2,
        out_specs=(hbm, hbm),
        scratch_shapes=[room(part.shape, part.dtype) for part in held] + [pltpu.SemaphoreType.DMA((2, 5))],
    )(*held)


def solution(mesh):
    placed = (
        P(("rec", "leaf", "rhs", "pan"), None),
        P(("rec", "leaf", "rhs", "pan"), None),
        P(("rec", "leaf", "rhs", "pan"), None),
        P("rec", ("leaf", "rhs", "pan")),
        P(("leaf", "rhs", "pan"), None),
        P(("leaf", "rhs", "pan")),
        P(("leaf", "rhs", "pan"), None),
        P(("rec", "leaf"), ("rhs", "pan")),
        P(("rec", "leaf"), None),
        P("rec", "leaf"),
        P(),
    )
    return jax.shard_map(
        shards,
        mesh=mesh,
        in_specs=placed,
        out_specs=(P(("rec", "leaf", "rhs", "pan"), None), P(("rec", "leaf", "rhs", "pan"), None)),
        check_vma=False,
    )
```

```python
import functools

import jax
import jax.numpy as jnp
from jax import lax
from jax.experimental import pallas as pl
from jax.experimental.pallas import tpu as pltpu
from jax.sharding import PartitionSpec as P

MESH = pl.DeviceIdType.MESH
F32 = jnp.float32
BF16 = jnp.bfloat16
LANES = 128
PLAIN = ((1,), (0,))
RIGHT_T = ((1,), (1,))
LEFT_T = ((0,), (0,))


def mul(a, b, dims=PLAIN):
    return lax.dot_general(a, b, (dims, ((), ())), preferred_element_type=F32)


def one_hot(rows, keys):
    shape = (rows, keys.shape[1])
    hit = lax.broadcasted_iota(jnp.int32, shape, 0) == keys
    return jnp.where(hit, 1.0, 0.0).astype(BF16)


def kernel(
    sizes,
    src_h, inv_h, upd_h, sen_h, ord_h, ext_h, tgt_h, us_h, ui_h, uc_h, ut_h,
    adj_h, grad_ref,
    src, inv, upd, sen, order, extent, target, us0, ui, uc, ut,
    local_sem,
    nhot, spread_upd, solved, ordered, adj,
    hi, us, iv, cp, ld, zed,
    sp, pr, lf, ba, back_own, gk, gs, gr, gh, gz,
    hi_s, hi_r, row_s, row_r, rel_s, rel_r, us_s, us_r, pr_s, pr_r, lf_s, lf_r, ba_s, ba_r, gr_s, gr_r, gz_s, gz_r,
):
    leaves, rhs, pan, front, rows_each = sizes
    members = rhs * pan
    depth = leaves.bit_length() - 1
    rows = inv.shape[0]
    width = us.shape[1]
    f = lax.axis_index("leaf")
    x = lax.axis_index("rhs")
    c = lax.axis_index("pan")
    j = x * pan + c
    half = front // 2
    inv_rows = ui.shape[0] - front
    cut = uc.shape[0] // 2
    upper_cols = uc.shape[1] - front
    strips = -(-upper_cols // LANES)
    part = hi.shape[1] // rhs

    def member(k):
        return lax.rem(j + k, members)

    def leaf(k):
        return lax.rem(f + k, leaves)

    def at_member(k):
        place = member(k)
        return {"rhs": place // pan, "pan": lax.rem(place, pan)}

    def at_leaf(k):
        return {"leaf": leaf(k)}

    def copy(a, b, s, r, to):
        return pltpu.make_async_remote_copy(
            src_ref=a, dst_ref=b, send_sem=s, recv_sem=r, device_id=to, device_id_type=MESH
        )

    fetch = {}
    for place, (name, a, b) in enumerate((
        ("ui", ui_h, ui), ("uc", uc_h, uc), ("order", ord_h, order), ("extent", ext_h, extent),
        ("target", tgt_h, target), ("ut", ut_h, ut), ("upd", upd_h, upd), ("src", src_h, src),
        ("inv", inv_h, inv), ("us0", us_h, us0), ("sen", sen_h, sen),
    )):
        fetch[name] = pltpu.make_async_copy(a, b, local_sem.at[place])
        if name in ("ui", "uc", "us0"):
            fetch[name].start()

    barrier = pltpu.get_barrier_semaphore()
    for k in range(1, members):
        pl.semaphore_signal(barrier, inc=1, device_id=at_member(k), device_id_type=MESH)
    for k in range(rhs, leaves * rhs):
        to = {"leaf": lax.rem(f + k // rhs, leaves), "rhs": lax.rem(x + k % rhs, rhs)}
        pl.semaphore_signal(barrier, inc=1, device_id=to, device_id_type=MESH)
    pl.semaphore_wait(barrier, members - 1 + (leaves - 1) * rhs)

    fetch["ui"].wait()
    fetch["uc"].wait()
    for side in range(2):
        slot = side * leaves + f
        hi[slot, 0:inv_rows, :] = ui[front:, side * half : (side + 1) * half]
        for strip in range(strips):
            start = inv_rows + strip * cut
            have = min(LANES, upper_cols - strip * LANES)
            piece = uc[side * cut : (side + 1) * cut, front + strip * LANES : front + strip * LANES + have]
            if have < LANES:
                piece = jnp.concatenate([piece, jnp.zeros((cut, LANES - have), BF16)], axis=1)
            hi[slot, start : start + cut, :] = piece
        start = inv_rows + strips * cut
        if start < hi.shape[1]:
            hi[slot, start:, :] = jnp.zeros((hi.shape[1] - start, LANES), BF16)
    sends = []

    def share(place):
        return hi.at[c * leaves + place, pl.ds(pl.multiple_of(x * part, part), part)]

    for k in range(1, leaves):
        out = copy(share(f), share(f), hi_s.at[k], hi_r.at[f], at_leaf(k))
        out.start()
        sends.append(out)
    fetch["us0"].wait()
    us[f] = us0[:, front:]
    for k in range(1, leaves):
        out = copy(us.at[f], us.at[f], us_s.at[k], us_r.at[f], at_leaf(k))
        out.start()
        sends.append(out)

    for name in ("order", "extent", "target", "ut", "src", "upd", "inv", "sen"):
        fetch[name].start()

    for name in ("order", "extent", "target", "ut"):
        fetch[name].wait()
    used = lax.broadcasted_iota(jnp.int32, (1, rows), 1) < extent[0]
    keys = jnp.where(used, order[...], -1)
    for start in range(0, rows, 256):
        hit = lax.broadcasted_iota(jnp.int32, (256, rows), 0) + start == keys
        nhot[start : start + 256, :] = jnp.where(hit, 1.0, 0.0).astype(BF16)
    fetch["src"].wait()
    ordered[...] = mul(src[...], nhot[...], LEFT_T).astype(BF16)
    fetch["upd"].wait()
    spread_upd[...] = mul(one_hot(front, target[...]), upd[...]).astype(BF16)
    fetch["inv"].wait()
    for start in range(0, rows, 256):
        end = start + 256
        block = mul(ordered[:, :end], inv[start:end, :end], RIGHT_T)
        solved[:, start:end] = jnp.where(used[:, start:end], block, 0.0).astype(BF16)
    sp[...] = mul(solved[...], spread_upd[...], RIGHT_T).astype(BF16)
    for k in range(1, members):
        to = pl.multiple_of(member(k) * width, width)
        out = copy(sp.at[pl.ds(to, width)], pr.at[j], pr_s.at[k], pr_r.at[j], at_member(k))
        out.start()
        sends.append(out)
    pr[j] = sp[pl.ds(pl.multiple_of(j * width, width), width), :]

    load_own = us0[:, :front].astype(F32)
    map_own = one_hot(front, ut[pl.ds(f, 1), :])
    cp_own = mul(map_own, uc[:, :front]).astype(BF16)
    inv_own = ui[:front, :]

    for k in range(1, leaves):
        g = leaf(k)
        copy(share(g), share(g), hi_s.at[k], hi_r.at[g], at_leaf(k)).wait_recv()
        for t in range(1, rhs):
            out = copy(share(g), share(g), row_s.at[t, k], row_r.at[x, g], {"rhs": lax.rem(x + t, rhs)})
            out.start()
            sends.append(out)

    for k in range(1, members):
        place = member(k)
        copy(pr.at[place], pr.at[place], pr_s.at[k], pr_r.at[place], at_member(k)).wait_recv()
    total = pr[0].astype(F32)
    for place in range(1, members):
        total = total + pr[place].astype(F32)
    front_in = (load_own - total).astype(BF16)
    zed_own = mul(front_in, inv_own, RIGHT_T).astype(BF16)
    lf[f] = mul(zed_own, cp_own, RIGHT_T).astype(BF16)
    for k in range(1, leaves):
        out = copy(lf.at[f], lf.at[f], lf_s.at[k], lf_r.at[f], at_leaf(k))
        out.start()
        sends.append(out)

    for k in range(1, leaves):
        slot = c * leaves + leaf(k)
        for t in range(1, rhs):
            other = lax.rem(x + t, rhs)
            here = hi.at[slot, pl.ds(pl.multiple_of(other * part, part), part)]
            copy(here, here, row_s.at[t, k], row_r.at[other, leaf(k)], {"rhs": other}).wait_recv()
        out = copy(hi.at[slot], hi.at[slot], rel_s.at[k], rel_r.at[leaf(k)], {"pan": 1 - c})
        out.start()
        sends.append(out)
    for k in range(1, leaves):
        slot = leaf(k)
        copy(us.at[slot], us.at[slot], us_s.at[k], us_r.at[slot], at_leaf(k)).wait_recv()
    for k in range(1, leaves):
        slot = (1 - c) * leaves + leaf(k)
        copy(hi.at[slot], hi.at[slot], rel_s.at[k], rel_r.at[leaf(k)], {"pan": 1 - c}).wait_recv()

    first = {}
    count = 0
    for height in range(1, depth + 1):
        first[height] = count
        count += leaves >> height
    for height in range(1, depth + 1):
        n = front >> height
        o = front - (2 * front >> height)
        for p in range(leaves >> height):
            at = first[height] + p
            group = [p * (1 << height) + s for s in range(1 << height)]
            for s, g in enumerate(group):
                for side in range(2):
                    iv[at, s * n : (s + 1) * n, side * half : (side + 1) * half] = hi[
                        side * leaves + g, o : o + n, :
                    ]
            if n % LANES == 0 and o % LANES == 0:
                ld[at] = jnp.concatenate([us[g, :, o : o + n] for g in group], axis=1).astype(F32)
            else:
                load = jnp.zeros(ld.shape[1:], F32)
                for s, g in enumerate(group):
                    line = lax.broadcasted_iota(jnp.int32, (1, front), 1) - s * n
                    line = jnp.where((line >= 0) & (line < n), line + o, -1)
                    load = load + mul(us[g], one_hot(us.shape[2], line))
                ld[at] = load
            if height < depth:
                pieces = []
                for s, g in enumerate(group):
                    strip_list = [
                        jnp.concatenate(
                            [
                                hi[side * leaves + g, inv_rows + strip * cut : inv_rows + (strip + 1) * cut, :]
                                for side in range(2)
                            ],
                            axis=0,
                        )
                        for strip in range(strips)
                    ]
                    if n % LANES == 0 and o % LANES == 0:
                        pieces.extend(strip_list[o // LANES : (o + n) // LANES])
                    else:
                        whole = jnp.concatenate(strip_list, axis=1)
                        line = lax.broadcasted_iota(jnp.int32, (1, front), 1) - s * n
                        line = jnp.where((line >= 0) & (line < n), line + o, -1)
                        gain = mul(whole, one_hot(whole.shape[1], line))
                        pieces = [gain + pieces[0]] if pieces else [gain]
                coup = jnp.concatenate(pieces, axis=1) if len(pieces) > 1 else pieces[0]
                map_row = 2 * leaves - (2 * leaves >> height) + p
                cp[at] = mul(one_hot(front, ut[map_row : map_row + 1, :]), coup.astype(BF16)).astype(BF16)

    for k in range(1, leaves):
        slot = leaf(k)
        copy(lf.at[slot], lf.at[slot], lf_s.at[k], lf_r.at[slot], at_leaf(k)).wait_recv()
    lifts = [lf[g].astype(F32) for g in range(leaves)]
    for height in range(1, depth + 1):
        above = []
        for p in range(leaves >> height):
            at = first[height] + p
            now = (ld[at] - (lifts[2 * p] + lifts[2 * p + 1])).astype(BF16)
            value = mul(now, iv[at], RIGHT_T).astype(BF16)
            zed[at] = value
            if height < depth:
                above.append(mul(value, cp[at], RIGHT_T))
        lifts = above
    back = mul(zed[first[depth]], iv[first[depth]]).astype(BF16)
    for height in range(depth - 1, 0, -1):
        at = first[height] + f // (1 << height)
        residue = (zed[at].astype(F32) - mul(back, cp[at])).astype(BF16)
        back = mul(residue, iv[at]).astype(BF16)
    residue = (zed_own.astype(F32) - mul(back, cp_own)).astype(BF16)
    back_own[...] = mul(residue, inv_own).astype(BF16)
    own_rows = pl.ds(pl.multiple_of(j * width, width), width)
    for k in range(1, members):
        out = copy(back_own, ba.at[own_rows], ba_s.at[k], ba_r.at[j], at_member(k))
        out.start()
        sends.append(out)
    ba[own_rows, :] = back_own[...]
    for k in range(1, members):
        place = member(k)
        here = ba.at[pl.ds(pl.multiple_of(place * width, width), width)]
        copy(here, here, ba_s.at[k], ba_r.at[place], at_member(k)).wait_recv()

    for start in range(0, rows, 256):
        end = start + 256
        value = solved[:, start:end].astype(F32) - mul(ba[...], spread_upd[:, start:end])
        ordered[:, start:end] = jnp.where(used[:, start:end], value, 0.0).astype(BF16)
    for start in range(0, rows, 256):
        end = start + 256
        block = mul(ordered[:, start:], inv[start:, start:end])
        solved[:, start:end] = jnp.where(used[:, start:end], block, 0.0).astype(BF16)
    adj[...] = mul(nhot[...], solved[...], RIGHT_T).astype(BF16)
    store = pltpu.make_async_copy(adj, adj_h, local_sem.at[11])
    store.start()
    fetch["sen"].wait()
    grad = -mul(sen[...], adj[...])
    tail = gs.shape[1] - rows_each

    def piece(g, place):
        start = (g * members + place) * rows_each
        value = grad[start : start + rows_each]
        if tail:
            value = jnp.concatenate([value, jnp.zeros((tail, value.shape[1]), F32)], axis=0)
        return value

    low = c == 0
    for g in range(leaves):
        for t in range(rhs):
            one, two = piece(g, t * pan), piece(g, t * pan + 1)
            gk[g * rhs + t] = jnp.where(low, one, two)
            gs[g * rhs + t] = jnp.where(low, two, one).astype(BF16)
    pair = copy(gs, gr, gr_s.at[0], gr_r.at[0], {"pan": 1 - c})
    pair.start()
    sends.append(pair)
    pair.wait_recv()
    gh[...] = (gk[...] + gr[...].astype(F32)).astype(BF16)
    here = f * rhs + x
    for k in range(1, leaves * rhs):
        g, t = lax.rem(f + k // rhs, leaves), lax.rem(x + k % rhs, rhs)
        out = copy(gh.at[g * rhs + t], gz.at[here], gz_s.at[k], gz_r.at[here], {"leaf": g, "rhs": t})
        out.start()
        sends.append(out)
    gz[here] = gh[here]
    for k in range(1, leaves * rhs):
        g, t = lax.rem(f + k // rhs, leaves), lax.rem(x + k % rhs, rhs)
        slot = g * rhs + t
        copy(gz.at[slot], gz.at[slot], gz_s.at[k], gz_r.at[slot], {"leaf": g, "rhs": t}).wait_recv()
    summed = gz[0].astype(F32)
    for slot in range(1, leaves * rhs):
        summed = summed + gz[slot].astype(F32)
    grad_ref[...] = summed[:rows_each]
    for out in sends:
        out.wait_send()
    store.wait()


def hand_on(adj, grad, adj_out, grad_out, adj_held, grad_held, sem):
    step = adj.shape[0] // 4
    parts = [(grad, grad_held, grad_out)]
    for start in range(0, adj.shape[0], step):
        rows = pl.ds(start, step)
        parts.append((adj.at[rows], adj_held.at[rows], adj_out.at[rows]))
    moves = []
    for place, (a, b, to) in enumerate(parts):
        come = pltpu.make_async_copy(a, b, sem.at[0, place])
        come.start()
        moves.append((come, pltpu.make_async_copy(b, to, sem.at[1, place])))
    for come, go in moves:
        come.wait()
        go.start()
    for come, go in moves:
        go.wait()


def shards(*arrays):
    (src, inv, upd, sen, order, extent, target, us, ui, uc, ut) = arrays
    us = us.T
    leaves, rhs, pan = (lax.axis_size(name) for name in ("leaf", "rhs", "pan"))
    members = rhs * pan
    front = ui.shape[1]
    rows, cols = src.shape
    width = cols // members
    rows_each = sen.shape[0] // (leaves * members)
    rows_kept = -(-rows_each // 16) * 16
    upper_rows = ui.shape[0] - front
    strips = -(-(uc.shape[1] - front) // LANES)
    hi_rows = -(-(upper_rows + strips * (uc.shape[0] // 2)) // (16 * rhs)) * 16 * rhs
    above = leaves - 1

    def room(shape, kind=BF16):
        return pltpu.VMEM(shape, kind)

    scratch = [
        room(src.shape), room(inv.shape), room(upd.shape), room(sen.shape),
        room(order.shape, jnp.int32), pltpu.SMEM(extent.shape, jnp.int32), room(target.shape, jnp.int32),
        room(us.shape), room(ui.shape), room(uc.shape), room(ut.shape, jnp.int32),
        pltpu.SemaphoreType.DMA((12,)),
        room((rows, rows)), room((front, rows)), room((cols, rows)), room((cols, rows)), room((rows, cols)),
        room((2 * leaves, hi_rows, LANES)), room((leaves, width, upper_rows)),
        room((above, front, front)), room((above, front, front)),
        room((above, width, front), F32), room((above, width, front)),
        room((cols, front)), room((members, width, front)), room((leaves, width, front)),
        room((cols, front)), room((width, front)),
        room((leaves * rhs, rows_kept, cols), F32), room((leaves * rhs, rows_kept, cols)),
        room((leaves * rhs, rows_kept, cols)), room((leaves * rhs, rows_kept, cols)),
        room((leaves * rhs, rows_kept, cols)),
    ]
    for count in (leaves, (rhs, leaves), leaves, leaves, members, leaves, members, 1, leaves * rhs):
        count = count if isinstance(count, tuple) else (count,)
        scratch += [pltpu.SemaphoreType.DMA(count)] * 2
    any_spec = pl.BlockSpec(memory_space=pl.ANY)
    hbm = pl.BlockSpec(memory_space=pltpu.HBM)
    flops = 2 * rows * rows * cols * 4
    held = pl.pallas_call(
        functools.partial(kernel, (leaves, rhs, pan, front, rows_each)),
        out_shape=(
            jax.ShapeDtypeStruct(src.shape, BF16),
            jax.ShapeDtypeStruct((rows_each, cols), F32),
        ),
        in_specs=[any_spec] * 11,
        out_specs=(any_spec, pl.BlockSpec(memory_space=pltpu.VMEM)),
        scratch_shapes=scratch,
        compiler_params=pltpu.CompilerParams(
            collective_id=0, has_side_effects=True, vmem_limit_bytes=56 * 2**20
        ),
        cost_estimate=pl.CostEstimate(flops=flops, bytes_accessed=5 * 2**20, transcendentals=0),
    )(src, inv, upd, sen, order, extent, target, us, ui, uc, ut)
    return pl.pallas_call(
        hand_on,
        out_shape=tuple(jax.ShapeDtypeStruct(part.shape, part.dtype) for part in held),
        in_specs=[hbm] * 2,
        out_specs=(hbm, hbm),
        scratch_shapes=[room(part.shape, part.dtype) for part in held] + [pltpu.SemaphoreType.DMA((2, 5))],
    )(*held)


def solution(mesh):
    placed = (
        P(("rec", "leaf", "rhs", "pan"), None),
        P(("rec", "leaf", "rhs", "pan"), None),
        P(("rec", "leaf", "rhs", "pan"), None),
        P("rec", ("leaf", "rhs", "pan")),
        P(("leaf", "rhs", "pan"), None),
        P(("leaf", "rhs", "pan")),
        P(("leaf", "rhs", "pan"), None),
        P(("rec", "leaf"), ("rhs", "pan")),
        P(("rec", "leaf"), None),
        P("rec", "leaf"),
        P(),
    )
    return jax.shard_map(
        shards,
        mesh=mesh,
        in_specs=placed,
        out_specs=(P(("rec", "leaf", "rhs", "pan"), None), P(("rec", "leaf", "rhs", "pan"), None)),
        check_vma=False,
    )
```

```python
import functools

import jax
import jax.numpy as jnp
from jax import lax
from jax.experimental import pallas as pl
from jax.experimental.pallas import tpu as pltpu
from jax.sharding import PartitionSpec as P

MESH = pl.DeviceIdType.MESH
F32 = jnp.float32
BF16 = jnp.bfloat16
LANES = 128
PLAIN = ((1,), (0,))
RIGHT_T = ((1,), (1,))
LEFT_T = ((0,), (0,))


def mul(a, b, dims=PLAIN):
    return lax.dot_general(a, b, (dims, ((), ())), preferred_element_type=F32)


def one_hot(rows, keys):
    shape = (rows, keys.shape[1])
    hit = lax.broadcasted_iota(jnp.int32, shape, 0) == keys
    return jnp.where(hit, 1.0, 0.0).astype(BF16)


def kernel(
    sizes,
    src_h, inv_h, upd_h, sen_h, ord_h, ext_h, tgt_h, us_h, ui_h, uc_h, ut_h,
    adj_h, grad_ref,
    src, inv, upd, sen, order, extent, target, us0, ui, uc, ut,
    local_sem,
    nhot, spread_upd, solved, ordered, adj,
    hi, us, iv, cp, ld, zed,
    sp, pr, lf, ba, back_own, gk, gs, gr, gh, gz,
    hi_s, hi_r, row_s, row_r, rel_s, rel_r, us_s, us_r, pr_s, pr_r, lf_s, lf_r, ba_s, ba_r, gr_s, gr_r, gz_s, gz_r,
):
    leaves, rhs, pan, front, rows_each = sizes
    members = rhs * pan
    depth = leaves.bit_length() - 1
    rows = inv.shape[0]
    width = us.shape[1]
    f = lax.axis_index("leaf")
    x = lax.axis_index("rhs")
    c = lax.axis_index("pan")
    j = x * pan + c
    half = front // 2
    inv_rows = ui.shape[0] - front
    cut = uc.shape[0] // 2
    upper_cols = uc.shape[1] - front
    strips = -(-upper_cols // LANES)
    part = hi.shape[1] // rhs

    def member(k):
        return lax.rem(j + k, members)

    def leaf(k):
        return lax.rem(f + k, leaves)

    def at_member(k):
        place = member(k)
        return {"rhs": place // pan, "pan": lax.rem(place, pan)}

    def at_leaf(k):
        return {"leaf": leaf(k)}

    def copy(a, b, s, r, to):
        return pltpu.make_async_remote_copy(
            src_ref=a, dst_ref=b, send_sem=s, recv_sem=r, device_id=to, device_id_type=MESH
        )

    fetch = {}
    for place, (name, a, b) in enumerate((
        ("ui", ui_h, ui), ("uc", uc_h, uc), ("order", ord_h, order), ("extent", ext_h, extent),
        ("target", tgt_h, target), ("ut", ut_h, ut), ("upd", upd_h, upd), ("src", src_h, src),
        ("inv", inv_h, inv), ("us0", us_h, us0), ("sen", sen_h, sen),
    )):
        fetch[name] = pltpu.make_async_copy(a, b, local_sem.at[place])
        if name in ("ui", "uc", "us0"):
            fetch[name].start()

    barrier = pltpu.get_barrier_semaphore()
    for k in range(1, members):
        pl.semaphore_signal(barrier, inc=1, device_id=at_member(k), device_id_type=MESH)
    for k in range(rhs, leaves * rhs):
        to = {"leaf": lax.rem(f + k // rhs, leaves), "rhs": lax.rem(x + k % rhs, rhs)}
        pl.semaphore_signal(barrier, inc=1, device_id=to, device_id_type=MESH)
    pl.semaphore_wait(barrier, members - 1 + (leaves - 1) * rhs)

    fetch["ui"].wait()
    fetch["uc"].wait()
    for side in range(2):
        slot = side * leaves + f
        hi[slot, 0:inv_rows, :] = ui[front:, side * half : (side + 1) * half]
        for strip in range(strips):
            start = inv_rows + strip * cut
            have = min(LANES, upper_cols - strip * LANES)
            piece = uc[side * cut : (side + 1) * cut, front + strip * LANES : front + strip * LANES + have]
            if have < LANES:
                piece = jnp.concatenate([piece, jnp.zeros((cut, LANES - have), BF16)], axis=1)
            hi[slot, start : start + cut, :] = piece
        start = inv_rows + strips * cut
        if start < hi.shape[1]:
            hi[slot, start:, :] = jnp.zeros((hi.shape[1] - start, LANES), BF16)
    sends = []

    def share(place):
        return hi.at[c * leaves + place, pl.ds(pl.multiple_of(x * part, part), part)]

    for k in range(1, leaves):
        out = copy(share(f), share(f), hi_s.at[k], hi_r.at[f], at_leaf(k))
        out.start()
        sends.append(out)
    fetch["us0"].wait()
    us[f] = us0[:, front:]
    for k in range(1, leaves):
        out = copy(us.at[f], us.at[f], us_s.at[k], us_r.at[f], at_leaf(k))
        out.start()
        sends.append(out)

    for name in ("order", "extent", "target", "ut", "src", "upd", "inv", "sen"):
        fetch[name].start()

    for name in ("order", "extent", "target", "ut"):
        fetch[name].wait()
    used = lax.broadcasted_iota(jnp.int32, (1, rows), 1) < extent[0]
    keys = jnp.where(used, order[...], -1)
    for start in range(0, rows, 256):
        hit = lax.broadcasted_iota(jnp.int32, (256, rows), 0) + start == keys
        nhot[start : start + 256, :] = jnp.where(hit, 1.0, 0.0).astype(BF16)
    fetch["src"].wait()
    ordered[...] = mul(src[...], nhot[...], LEFT_T).astype(BF16)
    fetch["upd"].wait()
    spread_upd[...] = mul(one_hot(front, target[...]), upd[...]).astype(BF16)
    fetch["inv"].wait()
    for start in range(0, rows, 256):
        end = start + 256
        block = mul(ordered[:, :end], inv[start:end, :end], RIGHT_T)
        solved[:, start:end] = jnp.where(used[:, start:end], block, 0.0).astype(BF16)
    sp[...] = mul(solved[...], spread_upd[...], RIGHT_T).astype(BF16)
    for k in range(1, members):
        to = pl.multiple_of(member(k) * width, width)
        out = copy(sp.at[pl.ds(to, width)], pr.at[j], pr_s.at[k], pr_r.at[j], at_member(k))
        out.start()
        sends.append(out)
    pr[j] = sp[pl.ds(pl.multiple_of(j * width, width), width), :]

    load_own = us0[:, :front].astype(F32)
    map_own = one_hot(front, ut[pl.ds(f, 1), :])
    cp_own = mul(map_own, uc[:, :front]).astype(BF16)
    inv_own = ui[:front, :]

    for k in range(1, members):
        place = member(k)
        copy(pr.at[place], pr.at[place], pr_s.at[k], pr_r.at[place], at_member(k)).wait_recv()
    total = pr[0].astype(F32)
    for place in range(1, members):
        total = total + pr[place].astype(F32)
    front_in = (load_own - total).astype(BF16)
    zed_own = mul(front_in, inv_own, RIGHT_T).astype(BF16)
    lf[f] = mul(zed_own, cp_own, RIGHT_T).astype(BF16)
    for k in range(1, leaves):
        out = copy(lf.at[f], lf.at[f], lf_s.at[k], lf_r.at[f], at_leaf(k))
        out.start()
        sends.append(out)

    for k in range(1, leaves):
        g = leaf(k)
        copy(share(g), share(g), hi_s.at[k], hi_r.at[g], at_leaf(k)).wait_recv()
        for t in range(1, rhs):
            out = copy(share(g), share(g), row_s.at[t, k], row_r.at[x, g], {"rhs": lax.rem(x + t, rhs)})
            out.start()
            sends.append(out)

    for k in range(1, leaves):
        slot = c * leaves + leaf(k)
        for t in range(1, rhs):
            other = lax.rem(x + t, rhs)
            here = hi.at[slot, pl.ds(pl.multiple_of(other * part, part), part)]
            copy(here, here, row_s.at[t, k], row_r.at[other, leaf(k)], {"rhs": other}).wait_recv()
        out = copy(hi.at[slot], hi.at[slot], rel_s.at[k], rel_r.at[leaf(k)], {"pan": 1 - c})
        out.start()
        sends.append(out)
    for k in range(1, leaves):
        slot = leaf(k)
        copy(us.at[slot], us.at[slot], us_s.at[k], us_r.at[slot], at_leaf(k)).wait_recv()
    for k in range(1, leaves):
        slot = (1 - c) * leaves + leaf(k)
        copy(hi.at[slot], hi.at[slot], rel_s.at[k], rel_r.at[leaf(k)], {"pan": 1 - c}).wait_recv()

    first = {}
    count = 0
    for height in range(1, depth + 1):
        first[height] = count
        count += leaves >> height
    for height in range(1, depth + 1):
        n = front >> height
        o = front - (2 * front >> height)
        for p in range(leaves >> height):
            at = first[height] + p
            group = [p * (1 << height) + s for s in range(1 << height)]
            for s, g in enumerate(group):
                for side in range(2):
                    iv[at, s * n : (s + 1) * n, side * half : (side + 1) * half] = hi[
                        side * leaves + g, o : o + n, :
                    ]
            if n % LANES == 0 and o % LANES == 0:
                ld[at] = jnp.concatenate([us[g, :, o : o + n] for g in group], axis=1).astype(F32)
            else:
                load = jnp.zeros(ld.shape[1:], F32)
                for s, g in enumerate(group):
                    line = lax.broadcasted_iota(jnp.int32, (1, front), 1) - s * n
                    line = jnp.where((line >= 0) & (line < n), line + o, -1)
                    load = load + mul(us[g], one_hot(us.shape[2], line))
                ld[at] = load
            if height < depth:
                pieces = []
                for s, g in enumerate(group):
                    strip_list = [
                        jnp.concatenate(
                            [
                                hi[side * leaves + g, inv_rows + strip * cut : inv_rows + (strip + 1) * cut, :]
                                for side in range(2)
                            ],
                            axis=0,
                        )
                        for strip in range(strips)
                    ]
                    if n % LANES == 0 and o % LANES == 0:
                        pieces.extend(strip_list[o // LANES : (o + n) // LANES])
                    else:
                        whole = jnp.concatenate(strip_list, axis=1)
                        line = lax.broadcasted_iota(jnp.int32, (1, front), 1) - s * n
                        line = jnp.where((line >= 0) & (line < n), line + o, -1)
                        gain = mul(whole, one_hot(whole.shape[1], line))
                        pieces = [gain + pieces[0]] if pieces else [gain]
                coup = jnp.concatenate(pieces, axis=1) if len(pieces) > 1 else pieces[0]
                map_row = 2 * leaves - (2 * leaves >> height) + p
                cp[at] = mul(one_hot(front, ut[map_row : map_row + 1, :]), coup.astype(BF16)).astype(BF16)

    for k in range(1, leaves):
        slot = leaf(k)
        copy(lf.at[slot], lf.at[slot], lf_s.at[k], lf_r.at[slot], at_leaf(k)).wait_recv()
    lifts = [lf[g].astype(F32) for g in range(leaves)]
    for height in range(1, depth + 1):
        above = []
        for p in range(leaves >> height):
            at = first[height] + p
            now = (ld[at] - (lifts[2 * p] + lifts[2 * p + 1])).astype(BF16)
            value = mul(now, iv[at], RIGHT_T).astype(BF16)
            zed[at] = value
            if height < depth:
                above.append(mul(value, cp[at], RIGHT_T))
        lifts = above
    back = mul(zed[first[depth]], iv[first[depth]]).astype(BF16)
    for height in range(depth - 1, 0, -1):
        at = first[height] + f // (1 << height)
        residue = (zed[at].astype(F32) - mul(back, cp[at])).astype(BF16)
        back = mul(residue, iv[at]).astype(BF16)
    residue = (zed_own.astype(F32) - mul(back, cp_own)).astype(BF16)
    back_own[...] = mul(residue, inv_own).astype(BF16)
    own_rows = pl.ds(pl.multiple_of(j * width, width), width)
    for k in range(1, members):
        out = copy(back_own, ba.at[own_rows], ba_s.at[k], ba_r.at[j], at_member(k))
        out.start()
        sends.append(out)
    ba[own_rows, :] = back_own[...]
    for k in range(1, members):
        place = member(k)
        here = ba.at[pl.ds(pl.multiple_of(place * width, width), width)]
        copy(here, here, ba_s.at[k], ba_r.at[place], at_member(k)).wait_recv()

    for start in range(0, rows, 256):
        end = start + 256
        value = solved[:, start:end].astype(F32) - mul(ba[...], spread_upd[:, start:end])
        ordered[:, start:end] = jnp.where(used[:, start:end], value, 0.0).astype(BF16)
    for start in range(0, rows, 256):
        end = start + 256
        block = mul(ordered[:, start:], inv[start:, start:end])
        solved[:, start:end] = jnp.where(used[:, start:end], block, 0.0).astype(BF16)
    adj[...] = mul(nhot[...], solved[...], RIGHT_T).astype(BF16)
    store = pltpu.make_async_copy(adj, adj_h, local_sem.at[11])
    store.start()
    fetch["sen"].wait()
    grad = -mul(sen[...], adj[...])
    tail = gs.shape[1] - rows_each

    def piece(g, place):
        start = (g * members + place) * rows_each
        value = grad[start : start + rows_each]
        if tail:
            value = jnp.concatenate([value, jnp.zeros((tail, value.shape[1]), F32)], axis=0)
        return value

    low = c == 0
    for g in range(leaves):
        for t in range(rhs):
            one, two = piece(g, t * pan), piece(g, t * pan + 1)
            gk[g * rhs + t] = jnp.where(low, one, two)
            gs[g * rhs + t] = jnp.where(low, two, one).astype(BF16)
    pair = copy(gs, gr, gr_s.at[0], gr_r.at[0], {"pan": 1 - c})
    pair.start()
    sends.append(pair)
    pair.wait_recv()
    gh[...] = (gk[...] + gr[...].astype(F32)).astype(BF16)
    here = f * rhs + x
    for k in range(1, leaves * rhs):
        g, t = lax.rem(f + k // rhs, leaves), lax.rem(x + k % rhs, rhs)
        out = copy(gh.at[g * rhs + t], gz.at[here], gz_s.at[k], gz_r.at[here], {"leaf": g, "rhs": t})
        out.start()
        sends.append(out)
    gz[here] = gh[here]
    for k in range(1, leaves * rhs):
        g, t = lax.rem(f + k // rhs, leaves), lax.rem(x + k % rhs, rhs)
        slot = g * rhs + t
        copy(gz.at[slot], gz.at[slot], gz_s.at[k], gz_r.at[slot], {"leaf": g, "rhs": t}).wait_recv()
    summed = gz[0].astype(F32)
    for slot in range(1, leaves * rhs):
        summed = summed + gz[slot].astype(F32)
    grad_ref[...] = summed[:rows_each]
    for out in sends:
        out.wait_send()
    store.wait()


def hand_on(adj, grad, adj_out, grad_out, adj_held, grad_held, sem):
    step = adj.shape[0] // 4
    parts = [(grad, grad_held, grad_out)]
    for start in range(0, adj.shape[0], step):
        rows = pl.ds(start, step)
        parts.append((adj.at[rows], adj_held.at[rows], adj_out.at[rows]))
    moves = []
    for place, (a, b, to) in enumerate(parts):
        come = pltpu.make_async_copy(a, b, sem.at[0, place])
        come.start()
        moves.append((come, pltpu.make_async_copy(b, to, sem.at[1, place])))
    for come, go in moves:
        come.wait()
        go.start()
    for come, go in moves:
        go.wait()


def shards(*arrays):
    (src, inv, upd, sen, order, extent, target, us, ui, uc, ut) = arrays
    us = us.T
    leaves, rhs, pan = (lax.axis_size(name) for name in ("leaf", "rhs", "pan"))
    members = rhs * pan
    front = ui.shape[1]
    rows, cols = src.shape
    width = cols // members
    rows_each = sen.shape[0] // (leaves * members)
    rows_kept = -(-rows_each // 16) * 16
    upper_rows = ui.shape[0] - front
    strips = -(-(uc.shape[1] - front) // LANES)
    hi_rows = -(-(upper_rows + strips * (uc.shape[0] // 2)) // (16 * rhs)) * 16 * rhs
    above = leaves - 1

    def room(shape, kind=BF16):
        return pltpu.VMEM(shape, kind)

    scratch = [
        room(src.shape), room(inv.shape), room(upd.shape), room(sen.shape),
        room(order.shape, jnp.int32), pltpu.SMEM(extent.shape, jnp.int32), room(target.shape, jnp.int32),
        room(us.shape), room(ui.shape), room(uc.shape), room(ut.shape, jnp.int32),
        pltpu.SemaphoreType.DMA((12,)),
        room((rows, rows)), room((front, rows)), room((cols, rows)), room((cols, rows)), room((rows, cols)),
        room((2 * leaves, hi_rows, LANES)), room((leaves, width, upper_rows)),
        room((above, front, front)), room((above, front, front)),
        room((above, width, front), F32), room((above, width, front)),
        room((cols, front)), room((members, width, front)), room((leaves, width, front)),
        room((cols, front)), room((width, front)),
        room((leaves * rhs, rows_kept, cols), F32), room((leaves * rhs, rows_kept, cols)),
        room((leaves * rhs, rows_kept, cols)), room((leaves * rhs, rows_kept, cols)),
        room((leaves * rhs, rows_kept, cols)),
    ]
    for count in (leaves, (rhs, leaves), leaves, leaves, members, leaves, members, 1, leaves * rhs):
        count = count if isinstance(count, tuple) else (count,)
        scratch += [pltpu.SemaphoreType.DMA(count)] * 2
    any_spec = pl.BlockSpec(memory_space=pl.ANY)
    hbm = pl.BlockSpec(memory_space=pltpu.HBM)
    flops = 2 * rows * rows * cols * 4
    held = pl.pallas_call(
        functools.partial(kernel, (leaves, rhs, pan, front, rows_each)),
        out_shape=(
            jax.ShapeDtypeStruct(src.shape, BF16),
            jax.ShapeDtypeStruct((rows_each, cols), F32),
        ),
        in_specs=[any_spec] * 11,
        out_specs=(any_spec, pl.BlockSpec(memory_space=pltpu.VMEM)),
        scratch_shapes=scratch,
        compiler_params=pltpu.CompilerParams(
            collective_id=0, has_side_effects=True, vmem_limit_bytes=56 * 2**20
        ),
        cost_estimate=pl.CostEstimate(flops=flops, bytes_accessed=5 * 2**20, transcendentals=0),
    )(src, inv, upd, sen, order, extent, target, us, ui, uc, ut)
    return pl.pallas_call(
        hand_on,
        out_shape=tuple(jax.ShapeDtypeStruct(part.shape, part.dtype) for part in held),
        in_specs=[hbm] * 2,
        out_specs=(hbm, hbm),
        scratch_shapes=[room(part.shape, part.dtype) for part in held] + [pltpu.SemaphoreType.DMA((2, 5))],
    )(*held)


def solution(mesh):
    placed = (
        P(("rec", "leaf", "rhs", "pan"), None),
        P(("rec", "leaf", "rhs", "pan"), None),
        P(("rec", "leaf", "rhs", "pan"), None),
        P("rec", ("leaf", "rhs", "pan")),
        P(("leaf", "rhs", "pan"), None),
        P(("leaf", "rhs", "pan")),
        P(("leaf", "rhs", "pan"), None),
        P(("rec", "leaf"), ("rhs", "pan")),
        P(("rec", "leaf"), None),
        P("rec", "leaf"),
        P(),
    )
    return jax.shard_map(
        shards,
        mesh=mesh,
        in_specs=placed,
        out_specs=(P(("rec", "leaf", "rhs", "pan"), None), P(("rec", "leaf", "rhs", "pan"), None)),
        check_vma=False,
    )
```
